32 devices in a mesh: rows: 8 (over z, core), ffn: 2 (over y), mp: 2 (over x).
Axes of the slice: x: 2, y: 2, z: 4, core: 2. Of those that a mesh axis runs over, the one named last changes fastest.
Arguments:
- query_rows: bfloat16 [512, 10240], P('rows', ('ffn', 'mp'))
- key_rows: bfloat16 [8192, 10240], P('rows', ('ffn', 'mp'))
- value_rows: bfloat16 [8192, 10240], P('rows', ('ffn', 'mp')), may hold values from -6 to 6
- seg_lengths: int32 [8, 5], P('rows'), may hold values from 1 to 256, 1024 in all within a row
- mask_pos: int32 [8, 64], P('rows'), may hold values from 0 to 1023, as said below
- residual_in: bfloat16 [512, 10240], P(('ffn', 'mp'), 'rows'), may hold values from -6 to 6
- out_weight: bfloat16 [10240, 10240], P(('ffn', 'mp'), 'rows'), may hold values from -0.0625 to 0.0625
- norm_gain: float32 [10240], P('rows'), may hold values from 0.25 to 1.75
- ffn_in_weight: bfloat16 [10240, 2, 31744], P('rows', None, ('ffn', 'mp')), may hold values from -0.0625 to 0.0625
- ffn_out_weight: bfloat16 [31744, 10240], P(('ffn', 'mp'), 'rows'), may hold values from -0.03125 to 0.03125
- final_gain: float32 [10240], P('rows'), may hold values from 0.25 to 1.75
- vocab_weight: bfloat16 [10240, 128], P('rows'), may hold values from -0.0625 to 0.0625
- targets: int32 [512], P(('ffn', 'mp')), may hold values from 0 to 127
Outputs:
- hidden_state: bfloat16 [512, 10240], P(('ffn', 'mp'), 'rows')
- log_probs: float32 [512], P(('ffn', 'mp'))
The draws below stay inside these ranges and needn't reach their ends.
Inputs may be any that keep to these rules, and one draw needn't show every extreme that they name: `mask_pos`: each masked slot's position within its packed row; slots of a row may repeat a position.
All inputs are finite; a program needn't handle non-finite values.
Results may differ from the reference program's by a relative error of at most 0.015.
Values may be sent and summed in bfloat16 or wider, within the bound.
No kernel may reach another device: no remote copies, remote signals or barrier semaphores. Data moves between devices by JAX's collectives and lax.ppermute only.
A program may use at most 256 MiB of HBM per device.

```python
import math
import jax
import jax.numpy as jnp
import numpy as np
from jax import lax

D = 10240
HEADS = 80
HD = 128
FF = 31744
VOCAB = 128
MOST = 256
ROW_LEN = 1024
MS = 64
SEGS = 5
TOKENS = 8192
MROWS = 512
N_ROWS = 8


def mask_positions(key):
    base_key = jax.random.fold_in(key, 7)
    slot_pos = jax.random.randint(base_key, (N_ROWS, MS), 0, ROW_LEN, dtype=jnp.int32)
    slot_pos = slot_pos.at[0, 0].set(ROW_LEN - 1)
    return slot_pos.at[0, 1].set(0)


def key_field(key):
    return jax.random.normal(jax.random.fold_in(key, 5), (TOKENS, HEADS * HD), jnp.float32)


def draw_mask_pos(key, part):
    slot_pos = mask_positions(key)
    return slot_pos


def draw_key_rows(key, part):
    field = key_field(key)
    return field.astype(jnp.bfloat16)


def draw_query_rows(key, part):
    key = jax.random.fold_in(key, 43)
    queries = jax.random.normal(key, (MROWS, HEADS * HD), jnp.float32)
    return queries.astype(jnp.bfloat16)


def set_ends(values, stream_key, low, top_value):
    index_at = [jax.random.randint(jax.random.fold_in(stream_key, axis), (), 0, length) for axis, length in enumerate(values.shape)]
    main_axis = values.shape.index(max(values.shape))
    beside = index_at[:main_axis] + [(index_at[main_axis] + 1) % values.shape[main_axis]] + index_at[main_axis + 1:]
    return values.at[tuple(index_at)].set(low).at[tuple(beside)].set(top_value)


def steps_of(stream_key, extent, cuts, least, top_value):
    level = 1.0
    for position, blocks in cuts:
        draws = jax.random.uniform(jax.random.fold_in(jax.random.fold_in(stream_key, 6), position), (blocks,), jnp.float32, least / len(cuts), top_value / len(cuts))
        level = level * jnp.repeat(jnp.exp(draws), extent[position] // blocks).reshape((-1,) + (1,) * (len(extent) - 1 - position))
    return level


def length_profile(amount, total, limit, lean):
    loads = [(1 << 20) // math.isqrt(grade ** lean) + 1 for grade in range(2, amount + 1)]
    spare, given = total - limit - (amount - 1), [1] * (amount - 1)
    while spare > 0:
        candidates = [i for i in range(amount - 1) if given[i] < limit]
        whole, left = sum([loads[i] for i in candidates]), spare
        for i in candidates:
            more = min(limit - given[i], max(1, left * loads[i] // whole), spare)
            given[i] = given[i] + more
            spare = spare - more
    return np.array([limit] + given)


def ragged_sizes(stream_key, amount, total, most, lean):
    if amount == 2:
        one = jax.random.randint(stream_key, (), max(1, total - most), min(most, total - 1) + 1)
        return jnp.stack([one, total - one])
    lengths = jnp.asarray(length_profile(amount, total, most, lean), jnp.int32)
    couples = (amount - 1) // 2
    giver, receiver = lengths[1:1 + 2 * couples:2], lengths[2:2 + 2 * couples:2]
    margin = jnp.minimum(giver - 1, most - receiver)
    passed = jax.random.randint(jax.random.fold_in(stream_key, 1), (couples,), 0, 1 << 20) % (margin + 1)
    lengths = lengths.at[1:1 + 2 * couples:2].set(giver - passed).at[2:2 + 2 * couples:2].set(receiver + passed)
    return lengths[jax.random.permutation(jax.random.fold_in(stream_key, 2), amount)]


def normal_values(own_key, extent, deviation, most, shards=(), kind=jnp.bfloat16):
    drawn = jax.random.normal(own_key, extent, jnp.float32) * deviation
    if len(shards) > 0:
        drawn = steps_of(own_key, extent, shards, -0.22, 0.18) * drawn
    return jnp.clip(drawn, min=-most, max=most).astype(kind)


def setup_inputs(seed: int = 0) -> dict:
    seeds = jax.random.split(jax.random.key(seed), 14)
    return {
        "query_rows": draw_query_rows(jax.random.fold_in(seeds[13], 71), 0),
        "key_rows": draw_key_rows(jax.random.fold_in(seeds[13], 71), 0),
        "value_rows": normal_values(seeds[2], (TOKENS, HEADS * HD), 1.0, 6.0, ((0, 8), (1, 4))),
        "seg_lengths": jax.vmap(lambda own: ragged_sizes(own, SEGS, ROW_LEN, MOST, 1))(jax.random.split(seeds[3], N_ROWS)).reshape((N_ROWS, SEGS)).astype(jnp.int32),
        "mask_pos": draw_mask_pos(jax.random.fold_in(seeds[13], 71), 0),
        "residual_in": normal_values(seeds[5], (MROWS, D), 1.0, 6.0, ((0, 4), (1, 8))),
        "out_weight": normal_values(seeds[6], (HEADS * HD, D), (HEADS * HD) ** -0.5, 0.0625, ((0, 4), (1, 8))),
        "norm_gain": jnp.clip(1.0 + 0.15 * jax.random.normal(seeds[7], (D,), jnp.float32), 0.25, 1.75),
        "ffn_in_weight": normal_values(seeds[8], (D, 2, FF), D ** -0.5, 0.0625, ((0, 8), (2, 4))),
        "ffn_out_weight": normal_values(seeds[9], (FF, D), FF ** -0.5, 0.03125, ((0, 4), (1, 8))),
        "final_gain": jnp.clip(1.0 + 0.15 * jax.random.normal(seeds[10], (D,), jnp.float32), 0.25, 1.75),
        "vocab_weight": normal_values(seeds[11], (D, VOCAB), D ** -0.5, 0.0625, ((0, 8),)),
        "targets": set_ends(jax.random.randint(seeds[12], (MROWS,), 0, VOCAB), jax.random.fold_in(seeds[12], 1), 0, VOCAB - 1).astype(jnp.int32),
    }


def row_attention(query_row, key_row, value_row, lengths_row, slot_pos):
    seg_ends = jnp.cumsum(lengths_row)
    token_index = jnp.arange(ROW_LEN, dtype=jnp.int32)
    token_seg = lax.optimization_barrier(jnp.sum((token_index[:, None] >= seg_ends[None, :]).astype(jnp.int32), axis=1))
    slot_seg = lax.optimization_barrier(jnp.sum((slot_pos[:, None] >= seg_ends[None, :]).astype(jnp.int32), axis=1))
    same_seg = slot_seg[:, None] == token_seg[None, :]
    query_heads = query_row.reshape(MS, HEADS, HD).astype(jnp.float32)
    key_heads = key_row.reshape(ROW_LEN, HEADS, HD).astype(jnp.float32)
    value_heads = value_row.reshape(ROW_LEN, HEADS, HD).astype(jnp.float32)
    scores = jnp.einsum('qhd,khd->hqk', query_heads, key_heads) * HD ** (-0.5)
    scores = jnp.where(same_seg[None, :, :], scores, -1e+30)
    top_score = lax.optimization_barrier(jnp.max(scores, axis=2, keepdims=True))
    exp_scores = jnp.exp(scores - top_score)
    score_total = lax.optimization_barrier(jnp.sum(exp_scores, axis=2, keepdims=True))
    weights = (exp_scores / score_total).astype(jnp.bfloat16)
    mixed = jnp.einsum('hqk,khd->qhd', weights.astype(jnp.float32), value_heads)
    return mixed.reshape(MS, HEADS * HD).astype(jnp.bfloat16)

def layer_norm(values_f32, gain):
    mean_val = lax.optimization_barrier(jnp.sum(values_f32, axis=1)) / D
    variance = lax.optimization_barrier(jnp.sum(values_f32 * values_f32, axis=1)) / D - mean_val * mean_val
    return ((values_f32 - mean_val[:, None]) * lax.rsqrt(variance + 1e-05)[:, None] * gain).astype(jnp.bfloat16)

def reference(query_rows, key_rows, value_rows, seg_lengths, mask_pos, residual_in, out_weight, norm_gain, ffn_in_weight, ffn_out_weight, final_gain, vocab_weight, targets):
    per_row = (query_rows.reshape(N_ROWS, MS, HEADS * HD), key_rows.reshape(N_ROWS, ROW_LEN, HEADS * HD), value_rows.reshape(N_ROWS, ROW_LEN, HEADS * HD), seg_lengths, mask_pos)
    head_out = lax.map(lambda item: row_attention(*item), per_row).reshape(MROWS, HEADS * HD)
    resid_mid = jnp.dot(head_out, out_weight, preferred_element_type=jnp.float32) + residual_in.astype(jnp.float32)
    normed_mid = layer_norm(resid_mid, norm_gain)
    both_units = jnp.dot(normed_mid, ffn_in_weight.reshape(D, 2 * FF), preferred_element_type=jnp.float32)
    act_units = (jax.nn.gelu(both_units[:, :FF], approximate=False) * both_units[:, FF:]).astype(jnp.bfloat16)
    hidden_state = (resid_mid + jnp.dot(act_units, ffn_out_weight, preferred_element_type=jnp.float32)).astype(jnp.bfloat16)
    normed_last = layer_norm(hidden_state.astype(jnp.float32), final_gain)
    logits = jnp.dot(normed_last, vocab_weight, preferred_element_type=jnp.float32)
    top_logit = lax.optimization_barrier(jnp.max(logits, axis=1, keepdims=True))
    log_total = jnp.log(lax.optimization_barrier(jnp.sum(jnp.exp(logits - top_logit), axis=1))) + top_logit[:, 0]
    vocab_index = jnp.arange(VOCAB, dtype=jnp.int32)
    picked = lax.optimization_barrier(jnp.sum(jnp.where(vocab_index[None, :] == targets[:, None], logits, 0.0), axis=1))
    return (hidden_state, picked - log_total)
```

```python
import functools

import jax
import jax.numpy as jnp
from jax import lax
from jax.experimental import pallas as pl
from jax.experimental.pallas import tpu as pltpu
from jax.sharding import PartitionSpec as P

HD = 128
GROUPS = 1
LAG = 2
F32 = jnp.float32
BF16 = jnp.bfloat16
VMEM_LIMIT = 20 * 1024 * 1024
BLOCK = 512
JOINT = 1
SMALL = pl.CostEstimate(flops=1024, bytes_accessed=1024, transcendentals=0)


def params(limit=None):
    return pltpu.CompilerParams(vmem_limit_bytes=limit or VMEM_LIMIT)


def anywhere():
    return pl.BlockSpec(memory_space=pl.ANY)


def in_smem():
    return pl.BlockSpec(memory_space=pltpu.SMEM)


def attention_kernel(heads, per_dot, seg_ref, pos_ref, query_ref, key_ref, value_ref, out_ref):
    row_len = key_ref.shape[0]
    token_index = lax.broadcasted_iota(jnp.int32, (1, row_len), 1)
    slot_pos = pos_ref[...]
    token_seg = jnp.zeros((1, row_len), jnp.int32)
    slot_seg = jnp.zeros(slot_pos.shape, jnp.int32)
    seg_end = jnp.int32(0)
    for pair in range(seg_ref.shape[1]):
        seg_end = seg_end + seg_ref[0, pair]
        token_seg = token_seg + (token_index >= seg_end).astype(jnp.int32)
        slot_seg = slot_seg + (slot_pos >= seg_end).astype(jnp.int32)
    same_seg = slot_seg == token_seg
    slots = slot_pos.shape[0]
    same_seg = jnp.concatenate([same_seg] * per_dot, axis=0)
    for first in range(0, heads, per_dot):
        cols = slice(first * HD, (first + per_dot) * HD)
        query = query_ref[:, cols]
        if per_dot == 2:
            blank = jnp.zeros((slots, HD), BF16)
            query = jnp.concatenate(
                [
                    jnp.concatenate([query[:, :HD], blank], axis=1),
                    jnp.concatenate([blank, query[:, HD:]], axis=1),
                ],
                axis=0,
            )
        scores = lax.dot_general(
            query, key_ref[:, cols], (((1,), (1,)), ((), ())), preferred_element_type=F32
        ) * HD ** (-0.5)
        scores = jnp.where(same_seg, scores, -1e30)
        exp_scores = jnp.exp(scores - jnp.max(scores, axis=1, keepdims=True))
        weights = (exp_scores / jnp.sum(exp_scores, axis=1, keepdims=True)).astype(BF16)
        mixed = jnp.dot(weights, value_ref[:, cols], preferred_element_type=F32).astype(BF16)
        for head in range(per_dot):
            out_ref[:, (first + head) * HD : (first + head + 1) * HD] = mixed[
                head * slots : (head + 1) * slots, head * HD : (head + 1) * HD
            ]


def attention(query_rows, key_rows, value_rows, seg_lengths, mask_pos):
    slots, width = query_rows.shape
    row_len = key_rows.shape[0]
    heads = max(h for h in (4, 2, 1) if (width // HD) % h == 0)
    block = heads * HD
    return pl.pallas_call(
        functools.partial(attention_kernel, heads, 2 if heads % 2 == 0 else 1),
        grid=(width // block,),
        in_specs=[
            in_smem(),
            pl.BlockSpec((slots, 1), lambda i: (0, 0)),
            pl.BlockSpec((slots, block), lambda i: (0, i)),
            pl.BlockSpec((row_len, block), lambda i: (0, i)),
            pl.BlockSpec((row_len, block), lambda i: (0, i)),
        ],
        out_specs=pl.BlockSpec((slots, block), lambda i: (0, i)),
        out_shape=jax.ShapeDtypeStruct((slots, width), BF16),
        compiler_params=params(60 * 1024 * 1024),
        cost_estimate=pl.CostEstimate(
            flops=4 * slots * row_len * width,
            bytes_accessed=4 * row_len * width,
            transcendentals=slots * row_len * width // HD,
        ),
    )(seg_lengths, mask_pos.reshape(slots, 1), query_rows, key_rows, value_rows)


def place_kernel(count, places_of, *refs):
    parts, out_ref, sem = refs[:count], refs[-2], refs[-1]
    copies = [
        pltpu.make_async_copy(part, out_ref.at[places_of(i)], sem.at[i]) for i, part in enumerate(parts)
    ]
    for copy in copies:
        copy.start()
    for copy in copies:
        copy.wait()


def place(parts, places_of, out_shape, after=()):
    return pl.pallas_call(
        functools.partial(place_kernel, len(parts), places_of),
        in_specs=[anywhere() for _ in (*parts, *after)],
        out_specs=anywhere(),
        out_shape=jax.ShapeDtypeStruct(out_shape, parts[0].dtype),
        scratch_shapes=[pltpu.SemaphoreType.DMA((len(parts),))],
        compiler_params=params(),
        cost_estimate=SMALL,
    )(*parts, *after)


def owner_permute(values, count, step):
    return lax.ppermute(values, ("ffn", "mp"), [(i, i ^ step) for i in range(count)])


def split_kernel(count, tokens, index_of, terms_ref, own_ref, *sent_refs):
    own_ref[...] = terms_ref[pl.ds(pl.multiple_of(index_of(0) * tokens, tokens), tokens), :]
    for step in range(1, count):
        start = pl.multiple_of(index_of(step) * tokens, tokens)
        sent_refs[step - 1][...] = terms_ref[pl.ds(start, tokens), :].astype(BF16)


def owner_sum(terms_f32, count, index_of):
    tokens, depth = terms_f32.shape[0] // count, terms_f32.shape[1]
    whole = pl.BlockSpec(memory_space=pltpu.VMEM)
    total, *sent = pl.pallas_call(
        functools.partial(split_kernel, count, tokens, index_of),
        in_specs=[whole],
        out_specs=[whole] * count,
        out_shape=[jax.ShapeDtypeStruct((tokens, depth), F32)]
        + [jax.ShapeDtypeStruct((tokens, depth), BF16)] * (count - 1),
        compiler_params=params(),
        cost_estimate=SMALL,
    )(terms_f32)
    for part in [owner_permute(sent[step - 1], count, step) for step in range(1, count)]:
        total = total + part.astype(F32)
    return total


def rows_sum(values, n_rows):
    spread = jnp.broadcast_to(values[None], (n_rows,) + values.shape)
    return jnp.sum(lax.all_to_all(spread, "rows", 0, 0).astype(F32), axis=0)


def layer_norm(values_f32, gain, n_rows):
    stats = jnp.stack([jnp.sum(values_f32, axis=1), jnp.sum(values_f32 * values_f32, axis=1)])
    stats = rows_sum(stats, n_rows)
    width = values_f32.shape[1] * n_rows
    mean_val = stats[0] / width
    variance = stats[1] / width - mean_val * mean_val
    scale = lax.rsqrt(variance + 1e-05)
    return ((values_f32 - mean_val[:, None]) * scale[:, None] * gain).astype(BF16)


def thirds(values):
    high = lax.reduce_precision(values, 8, 7)
    middle = lax.reduce_precision(values - high, 8, 7)
    low = values - high - middle
    return [part.astype(BF16) for part in (high, middle, low)]


def last_logits(values_f32, gain, vocab_weight, n_rows):
    tokens, width = values_f32.shape[0], values_f32.shape[1] * n_rows
    vocab = vocab_weight.shape[1]
    terms = jnp.dot((values_f32 * gain).astype(BF16), vocab_weight, preferred_element_type=F32)
    gain_terms = jnp.sum(gain[:, None] * vocab_weight.astype(F32), axis=0)
    sums, squares = jnp.sum(values_f32, axis=1), jnp.sum(values_f32 * values_f32, axis=1)
    room = max(tokens, vocab)
    extra = [
        jnp.pad(part, (0, room - part.shape[0]))
        for values in (sums, squares, gain_terms)
        for part in thirds(values)
    ]
    sent = jnp.concatenate([jnp.pad(terms.astype(BF16), ((0, 0), (0, room - vocab))), jnp.stack(extra)], axis=0)
    total = rows_sum(sent, n_rows)
    added = jnp.sum(total[tokens:].reshape(3, 3, room), axis=1)
    mean_val = added[0, :tokens] / width
    variance = added[1, :tokens] / width - mean_val * mean_val
    scale = lax.rsqrt(variance + 1e-05)
    return (total[:tokens, :vocab] - mean_val[:, None] * added[2, None, :vocab]) * scale[:, None]


def core_pairs(n_rows):
    return [(i, i ^ 1) for i in range(n_rows)]


def row_place():
    row = lax.axis_index("rows")
    return row // 2, row % 2


def gather_rows(values, n_rows, after):
    levels = n_rows // 2
    held = [values]
    for step in range(1, levels):
        pairs = [(i, (i - 2 * step) % n_rows) for i in range(n_rows)]
        held.append(lax.ppermute(values, "rows", pairs))
    mine = place(held, lambda i: (row_place()[0] + i) % levels, (levels,) + values.shape, after)
    other = lax.ppermute(mine, "rows", core_pairs(n_rows))
    both = place(
        [mine, other],
        lambda i: (slice(None), row_place()[1] ^ i),
        (levels, 2) + values.shape,
    )
    return both.reshape(n_rows * values.shape[0], values.shape[1])


def in_hbm():
    return pl.BlockSpec(memory_space=pltpu.HBM)


def in_vmem():
    return pl.BlockSpec(memory_space=pltpu.VMEM)


TOKEN = jax.ShapeDtypeStruct((8, 128), F32)


def distance():
    level, core = row_place()
    return jnp.where(core == 0, level, lax.axis_size("rows") // 2 - 1 - level)


def terms_kernel(slots, x_ref, w_ref, *rest):
    own_ref, twin_ref, token_ref = rest[-3:]
    token_ref[...] = jnp.zeros_like(token_ref)
    for part in range(2):
        terms = jnp.dot(x_ref[...], w_ref[part], preferred_element_type=F32)
        own_ref[0, part] = terms[:slots]
        twin_ref[0, part] = terms[slots:].astype(BF16)


def unit_terms(x, weights, block, count, width, after):
    rows, depth = x.shape
    slots = rows // 2
    sub = min(256, width)
    each = width // sub
    subs = min(count * each, -(-(weights.shape[2] - block * width) // sub))
    first = block * each

    def w_index(part):
        return (0, 0, first + part)

    def out_index(part):
        return (part // each, 0, 0, part % each)

    return pl.pallas_call(
        functools.partial(terms_kernel, slots),
        grid=(subs,),
        in_specs=[
            in_vmem(),
            pl.BlockSpec((2, depth, sub), w_index),
        ]
        + [anywhere() for _ in after],
        out_specs=[
            pl.BlockSpec((1, 2, slots, sub), out_index),
            pl.BlockSpec((1, 2, slots, sub), out_index),
            pl.BlockSpec((8, 128), lambda part: (0, 0)),
        ],
        out_shape=[
            jax.ShapeDtypeStruct((count, 2, slots, width), F32),
            jax.ShapeDtypeStruct((count, 2, slots, width), BF16),
            TOKEN,
        ],
        compiler_params=params(),
        cost_estimate=SMALL,
    )(x, weights, *after)


def relay_kernel(levels, choices, n_terms, n_after, has_terms, had_units, has_units, make_units, send_terms, *refs):
    refs = list(refs)
    owns, twins = refs[:n_terms], refs[n_terms : 2 * n_terms]
    del refs[: 2 * n_terms]
    got_ref = refs.pop(0) if has_terms else None
    made_ref = refs.pop(0) if has_units else None
    del refs[:n_after]
    out_ref, token_ref = refs.pop(0), refs.pop(0)
    units_ref = refs.pop(0) if make_units else None
    carry_ref = refs.pop(0) if has_units else None
    own_ref, twin_ref, sem = refs
    token_ref[...] = jnp.zeros_like(token_ref)
    where_at = distance()
    keep = None
    if has_units:
        at = 2 if send_terms else 0
        units = made_ref[...]
        if had_units:
            units = jnp.where(where_at == 0, units, got_ref[2])
        out_ref[at] = units
        keep = pltpu.make_async_copy(out_ref.at[at], carry_ref, sem.at[2])
        keep.start()
    for place_at in range(levels):
        if choices[place_at] is not None:

            @pl.when(where_at == place_at)
            def _(chosen=choices[place_at]):
                array, at = chosen
                own_copy = pltpu.make_async_copy(owns[array].at[at], own_ref, sem.at[0])
                twin_copy = pltpu.make_async_copy(twins[array].at[at], twin_ref, sem.at[1])
                own_copy.start()
                twin_copy.start()
                own_copy.wait()
                twin_copy.wait()

    sums = []
    for part in range(2):
        total = own_ref[part] + twin_ref[part].astype(F32)
        if has_terms:
            total = total + got_ref[part].astype(F32)
        sums.append(total)
        if send_terms:
            out_ref[part] = total.astype(BF16)
    if make_units:
        gate, up = sums

        @pl.when(where_at == levels - 1)
        def _():
            units_ref[...] = (0.5 * gate * (1.0 + lax.erf(gate * 0.5 ** 0.5)) * up).astype(BF16)

    if keep is not None:
        keep.wait()


def relay(levels, choices, flags, owns, twins, got, made, after):
    has_terms, had_units, has_units, make_units, send_terms = flags
    slots, width = owns[0].shape[2:]
    count = (2 if send_terms else 0) + (1 if has_units else 0)
    units = jax.ShapeDtypeStruct((slots, width), BF16)
    return pl.pallas_call(
        functools.partial(relay_kernel, levels, choices, len(owns), len(after), *flags),
        in_specs=[in_hbm() for _ in owns + twins]
        + [in_vmem() for _ in got + made]
        + [anywhere() for _ in after],
        out_specs=[in_vmem(), in_vmem()] + [in_vmem()] * make_units + [in_hbm()] * has_units,
        out_shape=[jax.ShapeDtypeStruct((count, slots, width), BF16), TOKEN]
        + [units] * make_units
        + [units] * has_units,
        scratch_shapes=[
            pltpu.VMEM((2, slots, width), F32),
            pltpu.VMEM((2, slots, width), BF16),
            pltpu.SemaphoreType.DMA((3,)),
        ],
        compiler_params=params(),
        cost_estimate=SMALL,
    )(*owns, *twins, *got, *made, *after)


def collect_kernel(levels, n_after, *refs):
    arrays, out_ref, sem = refs[:levels], refs[levels + n_after], refs[levels + n_after + 1]
    where_at = distance()
    for place_at in range(levels):

        @pl.when(where_at == place_at)
        def _(array=arrays[place_at]):
            copy = pltpu.make_async_copy(array, out_ref, sem)
            copy.start()
            copy.wait()


def collect(arrays, after):
    return pl.pallas_call(
        functools.partial(collect_kernel, len(arrays), len(after)),
        in_specs=[anywhere() for _ in arrays + after],
        out_specs=anywhere(),
        out_shape=jax.ShapeDtypeStruct(arrays[0].shape, BF16),
        scratch_shapes=[pltpu.SemaphoreType.DMA],
        compiler_params=params(),
        cost_estimate=SMALL,
    )(*arrays, *after)


def batches_of(blocks):
    sizes, left = [], blocks
    while left > 4:
        sizes.append(4)
        left -= 4
    while left > 1:
        sizes.append(left // 2)
        left -= left // 2
    return sizes + [left]


def shards(
    query_rows,
    key_rows,
    value_rows,
    seg_lengths,
    mask_pos,
    residual_in,
    out_weight,
    norm_gain,
    ffn_in_weight,
    ffn_out_weight,
    final_gain,
    vocab_weight,
    targets,
    *,
    n_rows,
    n_owners,
):
    levels = n_rows // 2
    slots = query_rows.shape[0]
    group_slots = slots // GROUPS
    owner_rows = n_rows // n_owners
    tokens = owner_rows * group_slots
    side_tokens = tokens * n_owners // 2
    depth = out_weight.shape[1]
    units = ffn_in_weight.shape[2]
    width = BLOCK if units >= 4096 else 256
    blocks = -(-units // width)
    pieces = GROUPS * blocks
    together = JOINT if blocks % JOINT == 0 else 1
    hops = LAG * (levels - 1)
    along = [(i, i + 2) for i in range(0, n_rows - 2, 2)] + [(i + 2, i) for i in range(1, n_rows - 2, 2)]

    def owner_at(step):
        return lax.axis_index("ffn") * lax.axis_size("mp") + lax.axis_index("mp") ^ step

    def position_at(step):
        return owner_at(step) ^ (row_place()[1] * (n_owners // 2))

    def of_group(values, group):
        split = values.reshape((owner_rows, GROUPS, group_slots) + values.shape[1:])
        return split[:, group].reshape((tokens,) + values.shape[1:])

    head_out = attention(query_rows, key_rows, value_rows, seg_lengths, mask_pos)
    unit_weights = jnp.transpose(ffn_in_weight, (1, 0, 2))

    resid_mid, x_groups = [], []
    for group in range(GROUPS):
        gathered = gather_rows(head_out[group * group_slots : (group + 1) * group_slots], n_rows, [unit_weights])
        attn_terms = jnp.dot(gathered, out_weight, preferred_element_type=F32)
        resid = owner_sum(attn_terms, n_owners, owner_at) + of_group(residual_in, group).astype(F32)
        normed = layer_norm(resid, norm_gain, n_rows)
        parts = [normed] + [owner_permute(normed, n_owners, step) for step in range(1, n_owners)]
        resid_mid.append(resid)
        x_groups.append(place(parts, position_at, (n_owners,) + normed.shape).reshape(-1, depth))

    last_term_step = pieces - 1 + hops
    last_step = last_term_step + 1 + hops
    own, twin, terms_token = {}, {}, {}

    def start_terms(piece, count, after):
        if piece < pieces and piece % count == 0:
            own[piece // together], sent, terms_token[piece - LAG] = unit_terms(
                x_groups[piece // blocks], unit_weights, piece % blocks, count, width, after
            )
            twin[piece // together] = lax.ppermute(sent, "rows", core_pairs(n_rows))

    for piece in range(0, LAG, together):
        start_terms(piece, together, [])

    got, carry, made, ready = {}, {}, {}, {}
    down_sums = [None] * GROUPS
    hidden, log_probs = [], []
    sizes = batches_of(blocks)
    ends = {sum(sizes[: i + 1]) - 1: size for i, size in enumerate(sizes)}

    def down_step(piece):
        group, block = piece // blocks, piece % blocks
        if block not in ends:
            return []
        count = ends[block]
        halves = [ready[p][half] for p in range(piece - count + 1, piece + 1) for half in range(2)]
        act = place(
            halves,
            lambda i: (
                pl.ds((i % 2) * side_tokens, side_tokens),
                pl.ds((i // 2) * width, width),
            ),
            (2 * side_tokens, count * width),
        )
        low = (block - count + 1) * width
        high = min((block + 1) * width, units)
        terms = jnp.dot(act[:, : high - low], ffn_out_weight[low:high], preferred_element_type=F32)
        down_sums[group] = terms if down_sums[group] is None else down_sums[group] + terms
        return [down_sums[group]]

    def finish(group):
        hidden_state = (resid_mid[group] + owner_sum(down_sums[group], n_owners, position_at)).astype(BF16)
        logits = last_logits(hidden_state.astype(F32), final_gain, vocab_weight, n_rows)
        top_logit = jnp.max(logits, axis=1, keepdims=True)
        log_total = jnp.log(jnp.sum(jnp.exp(logits - top_logit), axis=1)) + top_logit[:, 0]
        vocab_index = jnp.arange(logits.shape[1], dtype=jnp.int32)
        wanted = of_group(targets, group)
        picked = jnp.sum(jnp.where(vocab_index[None, :] == wanted[:, None], logits, 0.0), axis=1)
        hidden.append(hidden_state)
        log_probs.append(picked - log_total)

    after_down = []
    joint_got = None
    for step in range(last_step + 2 + LAG):
        if step <= last_term_step:
            choices = [step - LAG * d if 0 <= step - LAG * d < pieces else None for d in range(levels)]
            used = sorted({p // together for p in choices if p is not None})
            choices = [None if p is None else (used.index(p // together), p % together) for p in choices]
            has_terms = step >= LAG
            had_units = step >= hops + 1 + LAG
            has_units = step >= hops + 1
            make_units = step >= hops
            send_terms = step <= last_term_step - LAG
            out, token, *rest = relay(
                levels,
                choices,
                (has_terms, had_units, has_units, make_units, send_terms),
                [own[p] for p in used],
                [twin[p] for p in used],
                [got[step - LAG]] if has_terms else [],
                [made[step - 1]] if has_units else [],
                ([terms_token[step - 1]] if step - 1 in terms_token else []) + after_down,
            )
            got[step] = lax.ppermute(out, "rows", along)
            if make_units:
                made[step] = lax.ppermute(rest.pop(0), "rows", core_pairs(n_rows))
            if has_units:
                carry[step] = rest.pop(0)
            start_terms(step + LAG, together, [token])
        elif step <= last_step + LAG - 1:
            late = (step - last_term_step - 1) % LAG
            if step <= last_term_step + LAG:
                moved = got[step - LAG][-1]
                if late == 0:
                    moved = jnp.where(distance() == 0, made[step - 1], moved)
            else:
                moved = joint_got[late]
            carry[step] = moved
            if late == LAG - 1 and step <= last_step - LAG + LAG - 1:
                joint = jnp.stack([carry[step - LAG + 1 + i] for i in range(LAG)])
                joint_got = lax.ppermute(joint, "rows", along)
        piece = step - 2 * hops - 1
        if 0 <= piece < pieces:
            mine = collect([carry[piece + hops + 1 + LAG * d] for d in range(levels)], after_down)
            ready[piece] = (lax.ppermute(mine, "rows", core_pairs(n_rows)), mine)
        after_down = []
        piece = step - 2 * hops - 2
        if 0 <= piece < pieces:
            after_down = down_step(piece)
            if piece % blocks == blocks - 1:
                finish(piece // blocks)

    def joined(values):
        split = [v.reshape((owner_rows, group_slots) + v.shape[1:]) for v in values]
        return jnp.stack(split, axis=1).reshape((owner_rows * slots,) + values[0].shape[1:])

    return joined(hidden), joined(log_probs)


def solution(mesh):
    owners = ("ffn", "mp")
    in_specs = (
        P("rows", owners),
        P("rows", owners),
        P("rows", owners),
        P("rows", None),
        P("rows", None),
        P(owners, "rows"),
        P(owners, "rows"),
        P("rows"),
        P("rows", None, owners),
        P(owners, "rows"),
        P("rows"),
        P("rows", None),
        P(owners),
    )
    out_specs = (P(owners, "rows"), P(owners))
    body = functools.partial(
        shards, n_rows=mesh.shape["rows"], n_owners=mesh.shape["ffn"] * mesh.shape["mp"]
    )
    return jax.shard_map(body, mesh=mesh, in_specs=in_specs, out_specs=out_specs, check_vma=False)
```

```python
import functools

import jax
import jax.numpy as jnp
from jax import lax
from jax.experimental import pallas as pl
from jax.experimental.pallas import tpu as pltpu
from jax.sharding import PartitionSpec as P

HD = 128
GROUPS = 1
LAG = 2
F32 = jnp.float32
BF16 = jnp.bfloat16
VMEM_LIMIT = 20 * 1024 * 1024
BLOCK = 512
SMALL = pl.CostEstimate(flops=1024, bytes_accessed=1024, transcendentals=0)


def params(limit=None):
    return pltpu.CompilerParams(vmem_limit_bytes=limit or VMEM_LIMIT)


def anywhere():
    return pl.BlockSpec(memory_space=pl.ANY)


def in_smem():
    return pl.BlockSpec(memory_space=pltpu.SMEM)


def attention_kernel(heads, per_dot, seg_ref, pos_ref, query_ref, key_ref, value_ref, out_ref):
    row_len = key_ref.shape[0]
    token_index = lax.broadcasted_iota(jnp.int32, (1, row_len), 1)
    slots = pos_ref.shape[1]
    across = lax.broadcasted_iota(jnp.int32, (slots, slots), 0) == lax.broadcasted_iota(
        jnp.int32, (slots, slots), 1
    )
    slot_pos = jnp.sum(jnp.where(across, pos_ref[...], 0), axis=1, keepdims=True)
    token_seg = jnp.zeros((1, row_len), jnp.int32)
    slot_seg = jnp.zeros(slot_pos.shape, jnp.int32)
    seg_end = jnp.int32(0)
    for pair in range(seg_ref.shape[1]):
        seg_end = seg_end + seg_ref[0, pair]
        token_seg = token_seg + (token_index >= seg_end).astype(jnp.int32)
        slot_seg = slot_seg + (slot_pos >= seg_end).astype(jnp.int32)
    same_seg = slot_seg == token_seg
    same_seg = jnp.concatenate([same_seg] * per_dot, axis=0)
    for first in range(0, heads, per_dot):
        cols = slice(first * HD, (first + per_dot) * HD)
        query = query_ref[:, cols]
        if per_dot == 2:
            blank = jnp.zeros((slots, HD), BF16)
            query = jnp.concatenate(
                [
                    jnp.concatenate([query[:, :HD], blank], axis=1),
                    jnp.concatenate([blank, query[:, HD:]], axis=1),
                ],
                axis=0,
            )
        scores = lax.dot_general(
            query, key_ref[:, cols], (((1,), (1,)), ((), ())), preferred_element_type=F32
        ) * HD ** (-0.5)
        scores = jnp.where(same_seg, scores, -1e30)
        exp_scores = jnp.exp(scores - jnp.max(scores, axis=1, keepdims=True))
        weights = (exp_scores / jnp.sum(exp_scores, axis=1, keepdims=True)).astype(BF16)
        mixed = jnp.dot(weights, value_ref[:, cols], preferred_element_type=F32).astype(BF16)
        for head in range(per_dot):
            out_ref[:, (first + head) * HD : (first + head + 1) * HD] = mixed[
                head * slots : (head + 1) * slots, head * HD : (head + 1) * HD
            ]


def attention(query_rows, key_rows, value_rows, seg_lengths, mask_pos):
    slots, width = query_rows.shape
    row_len = key_rows.shape[0]
    heads = max(h for h in (4, 2, 1) if (width // HD) % h == 0)
    block = heads * HD
    return pl.pallas_call(
        functools.partial(attention_kernel, heads, 2 if heads % 2 == 0 else 1),
        grid=(width // block,),
        in_specs=[
            in_smem(),
            pl.BlockSpec((1, slots), lambda i: (0, 0)),
            pl.BlockSpec((slots, block), lambda i: (0, i)),
            pl.BlockSpec((row_len, block), lambda i: (0, i)),
            pl.BlockSpec((row_len, block), lambda i: (0, i)),
        ],
        out_specs=pl.BlockSpec((slots, block), lambda i: (0, i)),
        out_shape=jax.ShapeDtypeStruct((slots, width), BF16),
        compiler_params=params(60 * 1024 * 1024),
        cost_estimate=pl.CostEstimate(
            flops=4 * slots * row_len * width,
            bytes_accessed=4 * row_len * width,
            transcendentals=slots * row_len * width // HD,
        ),
    )(seg_lengths, mask_pos, query_rows, key_rows, value_rows)


def place_kernel(count, places_of, *refs):
    parts, out_ref, sem = refs[:count], refs[-2], refs[-1]
    copies = [
        pltpu.make_async_copy(part, out_ref.at[places_of(i)], sem.at[i]) for i, part in enumerate(parts)
    ]
    for copy in copies:
        copy.start()
    for copy in copies:
        copy.wait()


def place(parts, places_of, out_shape, after=()):
    return pl.pallas_call(
        functools.partial(place_kernel, len(parts), places_of),
        in_specs=[anywhere() for _ in (*parts, *after)],
        out_specs=anywhere(),
        out_shape=jax.ShapeDtypeStruct(out_shape, parts[0].dtype),
        scratch_shapes=[pltpu.SemaphoreType.DMA((len(parts),))],
        compiler_params=params(),
        cost_estimate=SMALL,
    )(*parts, *after)


def owner_permute(values, count, step):
    return lax.ppermute(values, ("ffn", "mp"), [(i, i ^ step) for i in range(count)])


def owner_gather(values, count, index_of):
    tokens, depth = values.shape
    shape = (count, tokens, depth)
    if count != 4 or depth % 256:
        parts = [values] + [owner_permute(values, count, step) for step in range(1, count)]
        return place(parts, index_of, shape).reshape(-1, depth)
    near = owner_permute(values, count, 1), owner_permute(values, count, 2)
    half = depth // 2
    far = (
        owner_permute(near[0][:, :half], count, 2),
        owner_permute(near[1][:, half:], count, 1),
    )

    def places_of(i):
        if i < 3:
            return index_of(i)
        return index_of(3), slice(None), pl.ds((i - 3) * half, half)

    return place([values, *near, *far], places_of, shape).reshape(-1, depth)


def split_kernel(count, tokens, index_of, terms_ref, own_ref, *sent_refs):
    own_ref[...] = terms_ref[pl.ds(pl.multiple_of(index_of(0) * tokens, tokens), tokens), :]
    for step in range(1, count):
        start = pl.multiple_of(index_of(step) * tokens, tokens)
        sent_refs[step - 1][...] = terms_ref[pl.ds(start, tokens), :].astype(BF16)


def owner_sum(terms_f32, count, index_of):
    tokens, depth = terms_f32.shape[0] // count, terms_f32.shape[1]
    whole = pl.BlockSpec(memory_space=pltpu.VMEM)
    total, *sent = pl.pallas_call(
        functools.partial(split_kernel, count, tokens, index_of),
        in_specs=[whole],
        out_specs=[whole] * count,
        out_shape=[jax.ShapeDtypeStruct((tokens, depth), F32)]
        + [jax.ShapeDtypeStruct((tokens, depth), BF16)] * (count - 1),
        compiler_params=params(),
        cost_estimate=SMALL,
    )(terms_f32)
    for part in [owner_permute(sent[step - 1], count, step) for step in range(1, count)]:
        total = total + part.astype(F32)
    return total


def rows_sum(values, n_rows):
    spread = jnp.broadcast_to(values[None], (n_rows,) + values.shape)
    return jnp.sum(lax.all_to_all(spread, "rows", 0, 0).astype(F32), axis=0)


def layer_norm(values_f32, gain, n_rows):
    stats = jnp.stack([jnp.sum(values_f32, axis=1), jnp.sum(values_f32 * values_f32, axis=1)])
    stats = rows_sum(stats, n_rows)
    width = values_f32.shape[1] * n_rows
    mean_val = stats[0] / width
    variance = stats[1] / width - mean_val * mean_val
    scale = lax.rsqrt(variance + 1e-05)
    return ((values_f32 - mean_val[:, None]) * scale[:, None] * gain).astype(BF16)


def thirds(values):
    high = lax.reduce_precision(values, 8, 7)
    middle = lax.reduce_precision(values - high, 8, 7)
    low = values - high - middle
    return [part.astype(BF16) for part in (high, middle, low)]


def last_logits(values_f32, gain, vocab_weight, n_rows):
    tokens, width = values_f32.shape[0], values_f32.shape[1] * n_rows
    vocab = vocab_weight.shape[1]
    terms = jnp.dot((values_f32 * gain).astype(BF16), vocab_weight, preferred_element_type=F32)
    gain_terms = jnp.sum(gain[:, None] * vocab_weight.astype(F32), axis=0)
    sums, squares = jnp.sum(values_f32, axis=1), jnp.sum(values_f32 * values_f32, axis=1)
    room = max(tokens, vocab)
    extra = [
        jnp.pad(part, (0, room - part.shape[0]))
        for values in (sums, squares, gain_terms)
        for part in thirds(values)
    ]
    sent = jnp.concatenate([jnp.pad(terms.astype(BF16), ((0, 0), (0, room - vocab))), jnp.stack(extra)], axis=0)
    total = rows_sum(sent, n_rows)
    added = jnp.sum(total[tokens:].reshape(3, 3, room), axis=1)
    mean_val = added[0, :tokens] / width
    variance = added[1, :tokens] / width - mean_val * mean_val
    scale = lax.rsqrt(variance + 1e-05)
    return (total[:tokens, :vocab] - mean_val[:, None] * added[2, None, :vocab]) * scale[:, None]


def core_pairs(n_rows):
    return [(i, i ^ 1) for i in range(n_rows)]


def row_place():
    row = lax.axis_index("rows")
    return row // 2, row % 2


def gather_rows(values, n_rows, after):
    levels = n_rows // 2
    held = [values]
    for step in range(1, levels):
        pairs = [(i, (i - 2 * step) % n_rows) for i in range(n_rows)]
        held.append(lax.ppermute(values, "rows", pairs))
    mine = place(held, lambda i: (row_place()[0] + i) % levels, (levels,) + values.shape, after)
    other = lax.ppermute(mine, "rows", core_pairs(n_rows))
    both = place(
        [mine, other],
        lambda i: (slice(None), row_place()[1] ^ i),
        (levels, 2) + values.shape,
    )
    return both.reshape(n_rows * values.shape[0], values.shape[1])


def in_hbm():
    return pl.BlockSpec(memory_space=pltpu.HBM)


def in_vmem():
    return pl.BlockSpec(memory_space=pltpu.VMEM)


TOKEN = jax.ShapeDtypeStruct((8, 128), F32)


def distance():
    level, core = row_place()
    return jnp.where(core == 0, level, lax.axis_size("rows") // 2 - 1 - level)


def terms_kernel(slots, x_ref, w_ref, *rest):
    own_ref, *twin_refs, token_ref = rest[-4:]
    token_ref[...] = jnp.zeros_like(token_ref)
    for part in range(2):
        terms = jnp.dot(x_ref[...], w_ref[part], preferred_element_type=F32)
        own_ref[part] = terms[:slots]
        twin_refs[part][...] = terms[slots:].astype(BF16)


def unit_terms(x, weights, block, width, after):
    rows, depth = x.shape
    slots = rows // 2
    sub = min(256, width)
    each = width // sub
    subs = min(each, -(-(weights.shape[2] - block * width) // sub))
    first = block * each

    def w_index(part):
        return (0, 0, first + part)

    def out_index(part):
        return (0, 0, part)

    return pl.pallas_call(
        functools.partial(terms_kernel, slots),
        grid=(subs,),
        in_specs=[
            in_vmem(),
            pl.BlockSpec((2, depth, sub), w_index),
        ]
        + [anywhere() for _ in after],
        out_specs=[
            pl.BlockSpec((2, slots, sub), out_index),
            pl.BlockSpec((slots, sub), lambda part: (0, part)),
            pl.BlockSpec((slots, sub), lambda part: (0, part)),
            pl.BlockSpec((8, 128), lambda part: (0, 0)),
        ],
        out_shape=[
            jax.ShapeDtypeStruct((2, slots, width), F32),
            jax.ShapeDtypeStruct((slots, width), BF16),
            jax.ShapeDtypeStruct((slots, width), BF16),
            TOKEN,
        ],
        compiler_params=params(),
        cost_estimate=SMALL,
    )(x, weights, *after)


def relay_kernel(levels, choices, n_terms, n_after, has_terms, had_units, has_units, make_units, send_terms, *refs):
    refs = list(refs)
    owns, twins = refs[:n_terms], refs[n_terms : 3 * n_terms]
    del refs[: 3 * n_terms]
    got_ref = refs.pop(0) if has_terms else None
    made_ref = refs.pop(0) if has_units else None
    del refs[:n_after]
    out_ref, token_ref = refs.pop(0), refs.pop(0)
    units_ref = refs.pop(0) if make_units else None
    carry_ref = refs.pop(0) if has_units else None
    own_ref, twin_ref, sem = refs
    token_ref[...] = jnp.zeros_like(token_ref)
    where_at = distance()
    keep = None
    if has_units:
        at = 2 if send_terms else 0
        units = made_ref[...]
        if had_units:
            units = jnp.where(where_at == 0, units, got_ref[2])
        out_ref[at] = units
        keep = pltpu.make_async_copy(out_ref.at[at], carry_ref, sem.at[3])
        keep.start()
    for place_at in range(levels):
        if choices[place_at] is not None:

            @pl.when(where_at == place_at)
            def _(chosen=choices[place_at]):
                copies = [pltpu.make_async_copy(owns[chosen], own_ref, sem.at[0])]
                for part in range(2):
                    twin = twins[2 * chosen + part]
                    copies.append(pltpu.make_async_copy(twin, twin_ref.at[part], sem.at[1 + part]))
                for copy in copies:
                    copy.start()
                for copy in copies:
                    copy.wait()

    sums = []
    for part in range(2):
        total = own_ref[part] + twin_ref[part].astype(F32)
        if has_terms:
            total = total + got_ref[part].astype(F32)
        sums.append(total)
        if send_terms:
            out_ref[part] = total.astype(BF16)
    if make_units:
        gate, up = sums

        @pl.when(where_at == levels - 1)
        def _():
            units_ref[...] = (0.5 * gate * (1.0 + lax.erf(gate * 0.5 ** 0.5)) * up).astype(BF16)

    if keep is not None:
        keep.wait()


def relay(levels, choices, flags, owns, twins, got, made, after):
    has_terms, had_units, has_units, make_units, send_terms = flags
    slots, width = owns[0].shape[1:]
    count = (2 if send_terms else 0) + (1 if has_units else 0)
    units = jax.ShapeDtypeStruct((slots, width), BF16)
    return pl.pallas_call(
        functools.partial(relay_kernel, levels, choices, len(owns), len(after), *flags),
        in_specs=[in_hbm() for _ in owns + twins]
        + [in_vmem() for _ in got + made]
        + [anywhere() for _ in after],
        out_specs=[in_vmem(), in_vmem()] + [in_vmem()] * make_units + [in_hbm()] * has_units,
        out_shape=[jax.ShapeDtypeStruct((count, slots, width), BF16), TOKEN]
        + [units] * make_units
        + [units] * has_units,
        scratch_shapes=[
            pltpu.VMEM((2, slots, width), F32),
            pltpu.VMEM((2, slots, width), BF16),
            pltpu.SemaphoreType.DMA((4,)),
        ],
        compiler_params=params(),
        cost_estimate=SMALL,
    )(*owns, *twins, *got, *made, *after)


def collect_kernel(levels, n_after, *refs):
    arrays, out_ref, sem = refs[:levels], refs[levels + n_after], refs[levels + n_after + 1]
    where_at = distance()
    for place_at in range(levels):

        @pl.when(where_at == place_at)
        def _(array=arrays[place_at]):
            copy = pltpu.make_async_copy(array, out_ref, sem)
            copy.start()
            copy.wait()


def collect(arrays, after):
    return pl.pallas_call(
        functools.partial(collect_kernel, len(arrays), len(after)),
        in_specs=[anywhere() for _ in arrays + after],
        out_specs=anywhere(),
        out_shape=jax.ShapeDtypeStruct(arrays[0].shape, BF16),
        scratch_shapes=[pltpu.SemaphoreType.DMA],
        compiler_params=params(),
        cost_estimate=SMALL,
    )(*arrays, *after)


def batches_of(blocks):
    sizes, left = [], blocks
    while left > 4:
        sizes.append(4)
        left -= 4
    while left > 2:
        sizes.append(2)
        left -= 2
    return sizes + [left]


def shards(
    query_rows,
    key_rows,
    value_rows,
    seg_lengths,
    mask_pos,
    residual_in,
    out_weight,
    norm_gain,
    ffn_in_weight,
    ffn_out_weight,
    final_gain,
    vocab_weight,
    targets,
    *,
    n_rows,
    n_owners,
):
    levels = n_rows // 2
    slots = query_rows.shape[0]
    group_slots = slots // GROUPS
    owner_rows = n_rows // n_owners
    tokens = owner_rows * group_slots
    side_tokens = tokens * n_owners // 2
    depth = out_weight.shape[1]
    units = ffn_in_weight.shape[2]
    width = BLOCK if units >= 4096 else 256
    blocks = -(-units // width)
    pieces = GROUPS * blocks
    last_width = units - (blocks - 1) * width
    hops = LAG * (levels - 1)
    along = [(i, i + 2) for i in range(0, n_rows - 2, 2)] + [(i + 2, i) for i in range(1, n_rows - 2, 2)]

    def owner_at(step):
        return lax.axis_index("ffn") * lax.axis_size("mp") + lax.axis_index("mp") ^ step

    def position_at(step):
        return owner_at(step) ^ (row_place()[1] * (n_owners // 2))

    def of_group(values, group):
        split = values.reshape((owner_rows, GROUPS, group_slots) + values.shape[1:])
        return split[:, group].reshape((tokens,) + values.shape[1:])

    head_out = attention(query_rows, key_rows, value_rows, seg_lengths, mask_pos)
    unit_weights = jnp.transpose(ffn_in_weight, (1, 0, 2))

    resid_mid, x_groups = [], []
    for group in range(GROUPS):
        gathered = gather_rows(head_out[group * group_slots : (group + 1) * group_slots], n_rows, [unit_weights])
        attn_terms = jnp.dot(gathered, out_weight, preferred_element_type=F32)
        resid = owner_sum(attn_terms, n_owners, owner_at) + of_group(residual_in, group).astype(F32)
        normed = layer_norm(resid, norm_gain, n_rows)
        resid_mid.append(resid)
        x_groups.append(owner_gather(normed, n_owners, position_at))

    last_term_step = pieces - 1 + hops
    last_step = last_term_step + 1 + hops
    own, twin, terms_token = {}, {}, {}

    def start_terms(piece, after):
        if piece < pieces:
            own[piece], *sent, terms_token[piece] = unit_terms(
                x_groups[piece // blocks], unit_weights, piece % blocks, width, after
            )
            twin[piece] = [lax.ppermute(part, "rows", core_pairs(n_rows)) for part in sent]

    for piece in range(LAG):
        start_terms(piece, [terms_token[piece - 1]] if piece else [])

    got, carry, made, ready = {}, {}, {}, {}
    down_sums = [None] * GROUPS
    hidden, log_probs = [], []
    sizes = batches_of(blocks)
    ends = {sum(sizes[: i + 1]) - 1: size for i, size in enumerate(sizes)}

    def down_step(piece):
        group, block = piece // blocks, piece % blocks
        if block not in ends:
            return []
        count = ends[block]
        halves = [ready[p][half] for p in range(piece - count + 1, piece + 1) for half in range(2)]
        act = place(
            halves,
            lambda i: (
                pl.ds((i % 2) * side_tokens, side_tokens),
                pl.ds((i // 2) * width, halves[i].shape[1]),
            ),
            (2 * side_tokens, (count - 1) * width + halves[-1].shape[1]),
        )
        low = (block - count + 1) * width
        high = min((block + 1) * width, units)
        terms = jnp.dot(act[:, : high - low], ffn_out_weight[low:high], preferred_element_type=F32)
        down_sums[group] = terms if down_sums[group] is None else down_sums[group] + terms
        return [down_sums[group]]

    def finish(group):
        hidden_state = (resid_mid[group] + owner_sum(down_sums[group], n_owners, position_at)).astype(BF16)
        logits = last_logits(hidden_state.astype(F32), final_gain, vocab_weight, n_rows)
        top_logit = jnp.max(logits, axis=1, keepdims=True)
        log_total = jnp.log(jnp.sum(jnp.exp(logits - top_logit), axis=1)) + top_logit[:, 0]
        vocab_index = jnp.arange(logits.shape[1], dtype=jnp.int32)
        wanted = of_group(targets, group)
        picked = jnp.sum(jnp.where(vocab_index[None, :] == wanted[:, None], logits, 0.0), axis=1)
        hidden.append(hidden_state)
        log_probs.append(picked - log_total)

    after_down = []
    final = []
    for step in range(last_step + 1):
        if step <= last_term_step:
            choices = [step - LAG * d if 0 <= step - LAG * d < pieces else None for d in range(levels)]
            used = sorted({p for p in choices if p is not None})
            choices = [None if p is None else used.index(p) for p in choices]
            has_terms = step >= LAG
            had_units = step >= hops + 1 + LAG
            has_units = step >= hops + 1
            make_units = step >= hops
            send_terms = step <= last_term_step - LAG
            out, token, *rest = relay(
                levels,
                choices,
                (has_terms, had_units, has_units, make_units, send_terms),
                [own[p] for p in used],
                [part for p in used for part in twin[p]],
                [got[step - LAG]] if has_terms else [],
                [made[step - 1]] if has_units else [],
                ([terms_token[step + 1]] if step + 1 in terms_token else []) + after_down,
            )
            got[step] = lax.ppermute(out, "rows", along)
            if make_units:
                made[step] = lax.ppermute(rest.pop(0), "rows", core_pairs(n_rows))
            if has_units:
                carry[step] = rest.pop(0)
            start_terms(step + LAG, [token])
        elif step < last_step:
            carry[step] = got[step - LAG][-1]
            if step == last_term_step + 1:
                kept = carry[step]
                carry[step] = place([kept], lambda i: 0, (1,) + kept.shape, [token])[0]
            if step < last_step - LAG:
                got[step] = lax.ppermute(carry[step][None], "rows", along)
            if step == last_term_step + 1:
                final = [made[step - 1][:, :last_width]]
                for place_at in range(1, levels):
                    pairs = [(0, 2 * place_at), (n_rows - 1, n_rows - 1 - 2 * place_at)]
                    final.append(lax.ppermute(final[0], "rows", pairs))
        piece = step - 2 * hops - 1
        if 0 <= piece < pieces - 1:
            if piece == pieces - 2:
                mine = collect(final, after_down)
                ready[pieces - 1] = (lax.ppermute(mine, "rows", core_pairs(n_rows)), mine)
            mine = collect([carry[piece + hops + 1 + LAG * d] for d in range(levels)], after_down)
            ready[piece] = (lax.ppermute(mine, "rows", core_pairs(n_rows)), mine)
        after_down = []
        piece = step - 2 * hops - 2
        if step == last_step:
            piece = pieces - 1
        if 0 <= piece < pieces:
            after_down = down_step(piece)
            if piece % blocks == blocks - 1:
                finish(piece // blocks)

    def joined(values):
        split = [v.reshape((owner_rows, group_slots) + v.shape[1:]) for v in values]
        return jnp.stack(split, axis=1).reshape((owner_rows * slots,) + values[0].shape[1:])

    return joined(hidden), joined(log_probs)


def solution(mesh):
    owners = ("ffn", "mp")
    in_specs = (
        P("rows", owners),
        P("rows", owners),
        P("rows", owners),
        P("rows", None),
        P("rows", None),
        P(owners, "rows"),
        P(owners, "rows"),
        P("rows"),
        P("rows", None, owners),
        P(owners, "rows"),
        P("rows"),
        P("rows", None),
        P(owners),
    )
    out_specs = (P(owners, "rows"), P(owners))
    body = functools.partial(
        shards, n_rows=mesh.shape["rows"], n_owners=mesh.shape["ffn"] * mesh.shape["mp"]
    )
    return jax.shard_map(body, mesh=mesh, in_specs=in_specs, out_specs=out_specs, check_vma=False)
```
